32 devices in a mesh: pole: 2 (over y), row: 4 (over z), col: 2 (over x), sub: 2 (over core).
Axes of the slice: x: 2, y: 2, z: 4, core: 2. Of those that a mesh axis runs over, the one named last changes fastest.
Arguments:
- ainv: bfloat16 [4, 256, 128, 128], P(('pole', 'col'), ('row', 'sub')), parts along dimension 0, may hold values from -6 to 6
- lfac: bfloat16 [192, 8, 128, 128], P(('pole', 'row', 'col'), 'sub'), parts along dimension 0, may hold values from -0.1875 to 0.1875
- anc: int32 [96, 8], P(('row', 'col')), may hold values from 0 to 15, as said below
- dinv: float32 [192, 128, 128], P(('pole', 'row', 'col', 'sub')), parts along dimension 0, may hold values from -6 to 6
Outputs:
- ancestor_inv: bfloat16 [192, 8, 128, 128], P(('pole', 'row', 'col'), 'sub'), parts along dimension 0
- diag_inv: float32 [192, 128, 128], P(('pole', 'row', 'col', 'sub')), parts along dimension 0
The draws below stay inside these ranges and needn't reach their ends.
There are 2 independent parts, one for each index of `pole`. The reference program is written for one: setup_inputs(seed, part) draws one part's arguments, and reference() takes and returns one part's arrays. A program takes and returns all parts, laid end to end along the dimension named above; an argument that names none is the same for every part. Nothing has to cross between parts.
Inputs may be any that keep to these rules, and one draw needn't show every extreme that they name: `anc`: each row lists 8 different ancestor indices in ascending order; its last 4 entries are always the subtree's top separators 16 - 4 .. 15.
All inputs are finite; a program needn't handle non-finite values.
Results may differ from the reference program's by a relative error of at most 0.0055.
Values may be sent and summed in bfloat16 or wider, within the bound.
A program may use at most 64 MiB of HBM per device.

```python
import jax
import jax.numpy as jnp
from jax import lax

B = 128
NANC = 16
M = 8
SN_GRP = 12
SUPER = 96
POOLS = 2


def draw_anc(key, part):
    key = jax.random.fold_in(key, 11)
    top_count = M // 2
    lower_count = NANC - top_count
    scores = jax.random.randint(key, (SUPER, lower_count), 0, 1 << 20) * lower_count + jnp.arange(lower_count, dtype=jnp.int32)[None, :]
    order = jnp.argsort(scores, axis=1)
    chosen = jnp.sort(order[:, :M - top_count], axis=1).astype(jnp.int32)
    tops = jnp.broadcast_to(jnp.arange(lower_count, NANC, dtype=jnp.int32)[None, :], (SUPER, top_count))
    return jnp.concatenate([chosen, tops], axis=1).astype(jnp.int32)


def levels(stream_key, dims, cuts, low, largest):
    loudness, own = 1.0, jax.random.fold_in(stream_key, 6)
    for position, shards_of in cuts:
        heights = jnp.exp(jax.random.uniform(jax.random.fold_in(own, position), (shards_of,), jnp.float32, low / len(cuts), largest / len(cuts)))
        loudness = loudness * jnp.repeat(heights, dims[position] // shards_of).reshape([-1 if axis == position else 1 for axis in range(len(dims))])
    return loudness


def bell_draw(own_key, shape, scale, most, pieces=(), kind=jnp.bfloat16):
    gain = levels(own_key, shape, pieces, -0.22, 0.18) if pieces else 1.0
    entries = jax.random.normal(own_key, shape, jnp.float32) * scale * gain
    return jnp.minimum(jnp.maximum(entries, -most), most).astype(kind)


def setup_inputs(seed: int = 0, part: int = 0) -> dict:
    key_of = jax.random.split(jax.random.key(seed), 5)
    part_splits = jax.random.split(jax.random.fold_in(key_of[4], part), 5)
    return {
        "ainv": bell_draw(part_splits[0], (POOLS, NANC * NANC, B, B), 1.0, 6.0, ((0, 2), (1, 8))),
        "lfac": bell_draw(part_splits[1], (SUPER, M, B, B), (M * B) ** -0.5, 0.1875, ((0, 8), (1, 2))),
        "anc": draw_anc(jax.random.fold_in(key_of[4], 71), part),
        "dinv": bell_draw(part_splits[3], (SUPER, B, B), 1.0, 6.0, ((0, 16),), jnp.float32),
    }


def reference(ainv, lfac, anc, dinv):
    pool_ids = ((jnp.arange(SUPER, dtype=jnp.int32) // SN_GRP) % POOLS).astype(jnp.int32)

    def one_supernode(args):
        ids, pool, panel, dinv_block = args
        flat = (ids[:, None] * NANC + ids[None, :]).astype(jnp.int32)
        table = lax.dynamic_index_in_dim(ainv, pool, 0, keepdims=False)
        blocks = table[flat.reshape(-1)].reshape(M, M, B, B)
        newblk = -jnp.einsum('ijab,jbc->iac', blocks.astype(jnp.float32), panel.astype(jnp.float32))
        rounded = newblk.astype(jnp.bfloat16)
        term = jnp.einsum('iba,ibc->ac', panel.astype(jnp.float32), rounded.astype(jnp.float32))
        return rounded, dinv_block - term

    ancestor_inv, diag_inv = lax.map(one_supernode, (anc, pool_ids, lfac, dinv))
    return ancestor_inv, diag_inv
```

```python
import functools

import jax
import jax.numpy as jnp
from jax import lax
from jax.experimental import pallas as pl
from jax.experimental.pallas import tpu as pltpu
from jax.sharding import PartitionSpec as P

NANC = 16
MESH = pl.DeviceIdType.MESH


def kernel(
    chips, anc_ref, ainv_ref, lfac_ref, dinv_ref, inv_ref, diag_ref,
    table, panel, outgoing, incoming, kept, recv, send, psem, tsem,
):
    z = lax.axis_index("row")
    sub = lax.axis_index("sub")
    other = 1 - sub
    supers, slots, width, _ = lfac_ref.shape
    owned = ainv_ref.shape[1]
    half = supers // 2
    pieces = recv.shape[1]
    mine = pieces // 2
    size = owned // mine
    chunk_blocks = 2 * owned
    lower = table.shape[0] // chunk_blocks
    base = sub * (NANC - slots) * NANC

    def ours(chunk):
        return jnp.where(sub == 0, chunk < lower, chunk >= lower)

    def place(core, chunk, piece):
        return pl.ds((chunk - core * lower) * chunk_blocks + piece * size, size)

    def hop(chunk, piece, step):
        where = table.at[place(sub, chunk, piece)]
        return pltpu.make_async_remote_copy(
            src_ref=where,
            dst_ref=where,
            send_sem=send.at[0 if step > 0 else 1, chunk, piece],
            recv_sem=recv.at[chunk, piece],
            device_id={"row": z + step},
            device_id_type=MESH,
        )

    def own_local(q):
        return pltpu.make_async_copy(
            ainv_ref.at[0, pl.ds(q * size, size)],
            table.at[place(sub, z, sub * mine + q)],
            recv.at[z, sub * mine + q],
        )

    def own_across(q):
        return pltpu.make_async_remote_copy(
            src_ref=ainv_ref.at[0, pl.ds(q * size, size)],
            dst_ref=table.at[place(other, z, sub * mine + q)],
            send_sem=send.at[0, z, sub * mine + q],
            recv_sem=recv.at[z, sub * mine + q],
            device_id={"sub": other},
            device_id_type=MESH,
        )

    panel_local = pltpu.make_async_copy(lfac_ref, panel.at[sub], psem.at[0])
    panel_across = pltpu.make_async_remote_copy(
        src_ref=lfac_ref,
        dst_ref=panel.at[sub],
        send_sem=psem.at[1],
        recv_sem=psem.at[2],
        device_id={"sub": other},
        device_id_type=MESH,
    )
    terms_across = pltpu.make_async_remote_copy(
        src_ref=outgoing,
        dst_ref=incoming,
        send_sem=tsem.at[0],
        recv_sem=tsem.at[1],
        device_id={"sub": other},
        device_id_type=MESH,
    )

    at_home = ours(z)

    @pl.when(at_home)
    def _():
        for q in range(mine):
            own_local(q).start()

    panel_local.start()

    barrier = pltpu.get_barrier_semaphore()
    pl.semaphore_signal(barrier, inc=1, device_id={"sub": other}, device_id_type=MESH)

    @pl.when(z > 0)
    def _():
        pl.semaphore_signal(barrier, inc=1, device_id={"row": z - 1}, device_id_type=MESH)

    @pl.when(z < chips - 1)
    def _():
        pl.semaphore_signal(barrier, inc=1, device_id={"row": z + 1}, device_id_type=MESH)

    pl.semaphore_wait(barrier, 1 + jnp.where(z > 0, 1, 0) + jnp.where(z < chips - 1, 1, 0))

    @pl.when(jnp.logical_not(at_home))
    def _():
        for q in range(mine):
            own_across(q).start()

    def arrived(chunk, piece):
        where = table.at[place(sub, chunk, piece)]
        pltpu.make_async_copy(where, where, recv.at[chunk, piece]).wait()

    @pl.when(at_home)
    def _():
        @pl.loop(0, pieces)
        def _(piece):
            arrived(z, piece)

            @pl.when(z < chips - 1)
            def _():
                hop(z, piece, 1).start()

            @pl.when(z > 0)
            def _():
                hop(z, piece, -1).start()

    panel_across.start()

    @pl.loop(pieces, chips * pieces)
    def _(n):
        t = lax.div(n, pieces)
        piece = lax.rem(n, pieces)
        up = z - t
        down = z + t

        @pl.when(jnp.logical_and(up >= 0, ours(up)))
        def _():
            arrived(up, piece)

            @pl.when(z < chips - 1)
            def _():
                hop(up, piece, 1).start()

        @pl.when(jnp.logical_and(down < chips, ours(down)))
        def _():
            arrived(down, piece)

            @pl.when(z > 0)
            def _():
                hop(down, piece, -1).start()

    panel_local.wait()
    panel_across.wait()

    def work(s):
        ids = [anc_ref[s, j] for j in range(2 * slots)]
        rows = [jnp.maximum(anc_ref[s, sub * slots + i] * NANC - base, 0) for i in range(slots)]
        total = None
        for j in range(0, 2 * slots, 2):
            left = jnp.concatenate(
                [
                    jnp.concatenate([table[row + ids[j]], table[row + ids[j + 1]]], axis=1)
                    for row in rows
                ],
                axis=0,
            )
            right = panel[j // slots, s, pl.ds(j % slots, 2)].reshape(2 * width, width)
            part = jnp.dot(left, right, preferred_element_type=jnp.float32)
            total = part if total is None else total + part
        made = (-total).astype(jnp.bfloat16)
        inv_ref[s] = made.reshape(slots, width, width)
        return lax.dot_general(
            panel[sub, s].reshape(slots * width, width),
            made,
            (((0,), (0,)), ((), ())),
            preferred_element_type=jnp.float32,
        )

    @pl.loop(0, half)
    def _(n):
        outgoing[n] = work(n + other * half).astype(jnp.bfloat16)

    terms_across.start()

    @pl.loop(0, half)
    def _(n):
        kept[n] = work(n + sub * half)

    terms_across.wait()
    diag_ref[...] = dinv_ref[...] - (kept[...] + incoming[...].astype(jnp.float32))

    @pl.when(jnp.logical_not(at_home))
    def _():
        for q in range(mine):
            own_across(q).wait_send()

    @pl.loop(0, chips * pieces)
    def _(n):
        t = lax.div(n, pieces)
        piece = lax.rem(n, pieces)
        up = z - t
        down = z + t

        @pl.when(jnp.logical_and(jnp.logical_and(up >= 0, ours(up)), z < chips - 1))
        def _():
            hop(up, piece, 1).wait_send()

        @pl.when(jnp.logical_and(jnp.logical_and(down < chips, ours(down)), z > 0))
        def _():
            hop(down, piece, -1).wait_send()


def shards(chips, ainv, lfac, anc, dinv):
    supers, slots, width, _ = lfac.shape
    owned = ainv.shape[1]
    pieces = 2 * max(1, owned // 8)
    kept_rows = (NANC - slots) * NANC
    half = supers // 2
    vmem = pl.BlockSpec(memory_space=pltpu.VMEM)
    hbm = pl.BlockSpec(memory_space=pl.ANY)
    return pl.pallas_call(
        functools.partial(kernel, chips),
        out_shape=(
            jax.ShapeDtypeStruct(lfac.shape, jnp.bfloat16),
            jax.ShapeDtypeStruct(dinv.shape, jnp.float32),
        ),
        in_specs=[pl.BlockSpec(memory_space=pltpu.SMEM), hbm, hbm, vmem],
        out_specs=(vmem, vmem),
        scratch_shapes=[
            pltpu.VMEM((kept_rows, width, width), jnp.bfloat16),
            pltpu.VMEM((2, supers, slots, width, width), jnp.bfloat16),
            pltpu.VMEM((half, width, width), jnp.bfloat16),
            pltpu.VMEM((half, width, width), jnp.bfloat16),
            pltpu.VMEM((half, width, width), jnp.float32),
            pltpu.SemaphoreType.DMA((chips, pieces)),
            pltpu.SemaphoreType.DMA((2, chips, pieces)),
            pltpu.SemaphoreType.DMA((3,)),
            pltpu.SemaphoreType.DMA((2,)),
        ],
        compiler_params=pltpu.CompilerParams(
            collective_id=0, has_side_effects=True, vmem_limit_bytes=40 * 1024 * 1024
        ),
        cost_estimate=pl.CostEstimate(
            flops=2 * supers * slots * (2 * slots + 1) * width**3,
            bytes_accessed=2 * (kept_rows + 4 * supers * slots) * width**2,
            transcendentals=0,
        ),
    )(anc, ainv, lfac, dinv)


def solution(mesh):
    return jax.shard_map(
        functools.partial(shards, mesh.shape["row"]),
        mesh=mesh,
        in_specs=(
            P(("pole", "col"), ("row", "sub"), None, None),
            P(("pole", "row", "col"), "sub", None, None),
            P(("row", "col"), None),
            P(("pole", "row", "col", "sub"), None, None),
        ),
        out_specs=(
            P(("pole", "row", "col"), "sub", None, None),
            P(("pole", "row", "col", "sub"), None, None),
        ),
        check_vma=False,
    )
```

```python
import functools

import jax
import jax.numpy as jnp
from jax import lax
from jax.experimental import pallas as pl
from jax.experimental.pallas import tpu as pltpu
from jax.sharding import PartitionSpec as P

NANC = 16
MESH = pl.DeviceIdType.MESH


def kernel(
    chips, anc_ref, ainv_ref, lfac_ref, dinv_ref, inv_ref, diag_ref,
    tops, lows, panel, turned, partial, dinv, outgoing, incoming, kept,
    recv_top, recv_low, send_top, send_low, psem, tsem,
):
    z = lax.axis_index("row")
    sub = lax.axis_index("sub")
    other = 1 - sub
    supers, slots, width, _ = lfac_ref.shape
    half = supers // 2
    quarters = NANC // slots
    split = NANC - slots
    lower = chips * split // NANC
    base = sub * split
    owned_rows, held, _, _ = ainv_ref.shape
    whole = held == NANC
    top_count = 2
    low_count = 2 * owned_rows

    def valid(top, chunk, i):
        if whole:
            return True
        last = lax.rem(chunk * 2 + i, quarters) == quarters - 1
        return last if top else jnp.logical_not(last)

    def owner(top, i):
        return i if top else lax.div(i, owned_rows)

    def ours(chunk):
        return jnp.where(sub == 0, chunk < lower, chunk >= lower)

    def place(top, core, chunk, i):
        if whole:
            row = chunk * 2 * owned_rows - core * split
            if top:
                return tops.at[pl.ds(row + i * owned_rows, owned_rows)]
            return lows.at[pl.ds(row + i, 1)]
        quarter = chunk * 2 + i
        row = lax.div(quarter, quarters) - core * split
        if top:
            return tops.at[pl.ds(row, 1)]
        return lows.at[pl.ds(row, 1), pl.ds(lax.rem(quarter, quarters) * slots, slots)]

    def source(top, i):
        if not whole:
            return ainv_ref
        if top:
            return ainv_ref.at[:, pl.ds(split, slots)]
        return ainv_ref.at[pl.ds(i - sub * owned_rows, 1), pl.ds(0, split)]

    def arrival(top, chunk, i):
        return (recv_top if top else recv_low).at[chunk, i]

    def departure(top, step, chunk, i):
        return (send_top if top else send_low).at[0 if step > 0 else 1, chunk, i]

    def hop(top, chunk, i, step):
        where = place(top, sub, chunk, i)
        return pltpu.make_async_remote_copy(
            src_ref=where,
            dst_ref=where,
            send_sem=departure(top, step, chunk, i),
            recv_sem=arrival(top, chunk, i),
            device_id={"row": z + step},
            device_id_type=MESH,
        )

    def own_local(top, i):
        return pltpu.make_async_copy(
            source(top, i), place(top, sub, z, i), arrival(top, z, i)
        )

    def own_across(top, i):
        return pltpu.make_async_remote_copy(
            src_ref=source(top, i),
            dst_ref=place(top, other, z, i),
            send_sem=departure(top, 1, z, i),
            recv_sem=arrival(top, z, i),
            device_id={"sub": other},
            device_id_type=MESH,
        )

    panel_local = pltpu.make_async_copy(lfac_ref, panel.at[sub], psem.at[0])
    panel_across = pltpu.make_async_remote_copy(
        src_ref=lfac_ref,
        dst_ref=panel.at[sub],
        send_sem=psem.at[1],
        recv_sem=psem.at[2],
        device_id={"sub": other},
        device_id_type=MESH,
    )
    dinv_local = pltpu.make_async_copy(dinv_ref, dinv, psem.at[3])
    terms_across = pltpu.make_async_remote_copy(
        src_ref=outgoing,
        dst_ref=incoming,
        send_sem=tsem.at[0],
        recv_sem=tsem.at[1],
        device_id={"sub": other},
        device_id_type=MESH,
    )

    at_home = ours(z)

    def each_own(action):
        for top, count in ((True, top_count), (False, low_count)):
            @pl.loop(0, count)
            def _(i):
                @pl.when(jnp.logical_and(valid(top, z, i), owner(top, i) == sub))
                def _():
                    action(top, i)

    @pl.when(at_home)
    def _():
        each_own(lambda top, piece: own_local(top, piece).start())

    barrier = pltpu.get_barrier_semaphore()
    pl.semaphore_signal(barrier, inc=1, device_id={"sub": other}, device_id_type=MESH)

    @pl.when(z > 0)
    def _():
        pl.semaphore_signal(barrier, inc=1, device_id={"row": z - 1}, device_id_type=MESH)

    @pl.when(z < chips - 1)
    def _():
        pl.semaphore_signal(barrier, inc=1, device_id={"row": z + 1}, device_id_type=MESH)

    pl.semaphore_wait(barrier, 1 + jnp.where(z > 0, 1, 0) + jnp.where(z < chips - 1, 1, 0))

    @pl.when(jnp.logical_not(at_home))
    def _():
        each_own(lambda top, piece: own_across(top, piece).start())

    def arrived(top, chunk, i):
        where = place(top, sub, chunk, i)
        pltpu.make_async_copy(where, where, arrival(top, chunk, i)).wait()

    @pl.when(at_home)
    def _():
        for top, count in ((True, top_count), (False, low_count)):
            @pl.loop(0, count)
            def _(i):
                @pl.when(valid(top, z, i))
                def _():
                    arrived(top, z, i)

                    @pl.when(z < chips - 1)
                    def _():
                        hop(top, z, i, 1).start()

                    @pl.when(z > 0)
                    def _():
                        hop(top, z, i, -1).start()

    panel_local.start()
    panel_across.start()
    dinv_local.start()

    def relay(top, t, i):
        up = z - t
        down = z + t

        @pl.when(jnp.logical_and(jnp.logical_and(up >= 0, ours(up)), valid(top, up, i)))
        def _():
            arrived(top, up, i)

            @pl.when(z < chips - 1)
            def _():
                hop(top, up, i, 1).start()

        @pl.when(jnp.logical_and(jnp.logical_and(down < chips, ours(down)), valid(top, down, i)))
        def _():
            arrived(top, down, i)

            @pl.when(z > 0)
            def _():
                hop(top, down, i, -1).start()

    panel_local.wait()

    @pl.loop(0, supers)
    def _(s):
        turned[s] = panel[sub, s].reshape(slots * width, width).T

    panel_across.wait()

    def multiply(table, first, s):
        rows = [
            jnp.maximum(anc_ref[sub * slots + i, s] - base, 0) for i in range(slots)
        ]
        ids = [anc_ref[first * slots + j, s] for j in range(slots)]
        if first:
            ids = [jnp.maximum(b - (NANC - slots), 0) for b in ids]
        total = None
        for j in range(0, slots, 2):
            left = jnp.concatenate(
                [
                    jnp.concatenate([table[row, ids[j]], table[row, ids[j + 1]]], axis=1)
                    for row in rows
                ],
                axis=0,
            )
            right = panel[first, s, pl.ds(j, 2)].reshape(2 * width, width)
            part = jnp.dot(left, right, preferred_element_type=jnp.float32)
            total = part if total is None else total + part
        return total

    first_mine = sub * lower
    last_mine = jnp.where(sub == 0, lower, chips) - 1
    final = jnp.maximum(jnp.maximum(z - first_mine, last_mine - z), 1)
    share = -(-supers // low_count)

    @pl.loop(1, chips)
    def _(t):
        @pl.loop(0, top_count)
        def _(i):
            relay(True, t, i)

        @pl.loop(0, low_count)
        def _(i):
            @pl.when(t == final)
            def _():
                @pl.loop(0, share)
                def _(k):
                    s = i * share + k

                    @pl.when(s < supers)
                    def _():
                        partial[s] = multiply(tops, 1, s)

            relay(False, t, i)

    def work(s):
        made = (-(partial[s] + multiply(lows, 0, s))).astype(jnp.bfloat16)
        inv_ref[s] = made.reshape(slots, width, width)
        return jnp.dot(turned[s], made, preferred_element_type=jnp.float32)

    together = 2 if half % 2 == 0 else 1

    @pl.loop(0, half // together)
    def _(m):
        for u in range(together):
            n = m * together + u
            outgoing[n] = work(n + other * half).astype(jnp.bfloat16)

    terms_across.start()

    @pl.loop(0, half // together)
    def _(m):
        for u in range(together):
            n = m * together + u
            kept[n] = work(n + sub * half)

    dinv_local.wait()
    terms_across.wait()
    diag_ref[...] = dinv[...] - (kept[...] + incoming[...].astype(jnp.float32))

    @pl.when(jnp.logical_not(at_home))
    def _():
        each_own(lambda top, piece: own_across(top, piece).wait_send())

    @pl.loop(0, chips)
    def _(t):
        up = z - t
        down = z + t
        go_up = jnp.logical_and(jnp.logical_and(up >= 0, ours(up)), z < chips - 1)
        go_down = jnp.logical_and(jnp.logical_and(down < chips, ours(down)), z > 0)
        for top, count in ((True, top_count), (False, low_count)):
            @pl.loop(0, count)
            def _(i):
                @pl.when(jnp.logical_and(go_up, valid(top, up, i)))
                def _():
                    hop(top, up, i, 1).wait_send()

                @pl.when(jnp.logical_and(go_down, valid(top, down, i)))
                def _():
                    hop(top, down, i, -1).wait_send()


def shards(chips, ainv, lfac, anc, dinv):
    supers, slots, width, _ = lfac.shape
    owned = ainv.shape[1]
    held = min(owned, NANC)
    pieces = 2 * (owned // held)
    kept_rows = (NANC - slots) * NANC
    half = supers // 2
    vmem = pl.BlockSpec(memory_space=pltpu.VMEM)
    hbm = pl.BlockSpec(memory_space=pltpu.HBM)
    return pl.pallas_call(
        functools.partial(kernel, chips),
        out_shape=(
            pltpu.VMEM(lfac.shape, jnp.bfloat16),
            pltpu.VMEM(dinv.shape, jnp.float32),
        ),
        in_specs=[pl.BlockSpec(memory_space=pltpu.SMEM), hbm, hbm, hbm],
        out_specs=(vmem, vmem),
        scratch_shapes=[
            pltpu.VMEM((NANC - slots, slots, width, width), jnp.bfloat16),
            pltpu.VMEM((NANC - slots, NANC - slots, width, width), jnp.bfloat16),
            pltpu.VMEM((2, supers, slots, width, width), jnp.bfloat16),
            pltpu.VMEM((supers, width, slots * width), jnp.bfloat16),
            pltpu.VMEM((supers, slots * width, width), jnp.float32),
            pltpu.VMEM(dinv.shape, jnp.float32),
            pltpu.VMEM((half, width, width), jnp.bfloat16),
            pltpu.VMEM((half, width, width), jnp.bfloat16),
            pltpu.VMEM((half, width, width), jnp.float32),
            pltpu.SemaphoreType.DMA((chips, 2)),
            pltpu.SemaphoreType.DMA((chips, pieces)),
            pltpu.SemaphoreType.DMA((2, chips, 2)),
            pltpu.SemaphoreType.DMA((2, chips, pieces)),
            pltpu.SemaphoreType.DMA((4,)),
            pltpu.SemaphoreType.DMA((2,)),
        ],
        compiler_params=pltpu.CompilerParams(
            collective_id=0, has_side_effects=True, vmem_limit_bytes=60 * 1024 * 1024
        ),
        cost_estimate=pl.CostEstimate(
            flops=2 * supers * slots * (2 * slots + 1) * width**3,
            bytes_accessed=2 * (kept_rows + 4 * supers * slots) * width**2,
            transcendentals=0,
        ),
    )(anc.T, ainv.reshape(owned // held, held, width, width), lfac, dinv)


def solution(mesh):
    return jax.shard_map(
        functools.partial(shards, mesh.shape["row"]),
        mesh=mesh,
        in_specs=(
            P(("pole", "col"), ("row", "sub"), None, None),
            P(("pole", "row", "col"), "sub", None, None),
            P(("row", "col"), None),
            P(("pole", "row", "col", "sub"), None, None),
        ),
        out_specs=(
            P(("pole", "row", "col"), "sub", None, None),
            P(("pole", "row", "col", "sub"), None, None),
        ),
        check_vma=False,
    )
```

```python
import functools

import jax
import jax.numpy as jnp
from jax import lax
from jax.experimental import pallas as pl
from jax.experimental.pallas import tpu as pltpu
from jax.sharding import PartitionSpec as P

NANC = 16
MESH = pl.DeviceIdType.MESH


def kernel(
    chips, anc_ref, ainv_ref, lfac_ref, dinv_ref, inv_ref, diag_ref,
    tops, lows, panel, turned, partial, dinv, outgoing, incoming, kept,
    recv_top, recv_low, send_top, send_low, psem, tsem,
):
    z = lax.axis_index("row")
    sub = lax.axis_index("sub")
    other = 1 - sub
    supers, slots, width, _ = lfac_ref.shape
    half = supers // 2
    quarters = NANC // slots
    split = NANC - slots
    lower = chips * split // NANC
    base = sub * split
    owned_rows, held, _, _ = ainv_ref.shape
    whole = held == NANC
    top_count = 2
    low_count = 2 * owned_rows

    def valid(top, chunk, i):
        if whole:
            return True
        last = lax.rem(chunk * 2 + i, quarters) == quarters - 1
        return last if top else jnp.logical_not(last)

    def owner(top, i):
        return i if top else lax.div(i, owned_rows)

    def ours(chunk):
        return jnp.where(sub == 0, chunk < lower, chunk >= lower)

    def place(top, core, chunk, i):
        if whole:
            row = chunk * 2 * owned_rows - core * split
            if top:
                return tops.at[pl.ds(row + i * owned_rows, owned_rows)]
            return lows.at[pl.ds(row + i, 1)]
        quarter = chunk * 2 + i
        row = lax.div(quarter, quarters) - core * split
        if top:
            return tops.at[pl.ds(row, 1)]
        return lows.at[pl.ds(row, 1), pl.ds(lax.rem(quarter, quarters) * slots, slots)]

    def source(top, i):
        if not whole:
            return ainv_ref
        if top:
            return ainv_ref.at[:, pl.ds(split, slots)]
        return ainv_ref.at[pl.ds(i - sub * owned_rows, 1), pl.ds(0, split)]

    def arrival(top, chunk, i):
        return (recv_top if top else recv_low).at[chunk, i]

    def departure(top, step, chunk, i):
        return (send_top if top else send_low).at[0 if step > 0 else 1, chunk, i]

    def hop(top, chunk, i, step, origin=None):
        where = place(top, sub, chunk, i)
        return pltpu.make_async_remote_copy(
            src_ref=where if origin is None else origin,
            dst_ref=where,
            send_sem=departure(top, step, chunk, i),
            recv_sem=arrival(top, chunk, i),
            device_id={"row": z + step},
            device_id_type=MESH,
        )

    def own_local(top, i):
        return pltpu.make_async_copy(
            source(top, i), place(top, sub, z, i), arrival(top, z, i)
        )

    def own_across(top, i):
        return pltpu.make_async_remote_copy(
            src_ref=source(top, i),
            dst_ref=place(top, other, z, i),
            send_sem=departure(top, 1, z, i),
            recv_sem=arrival(top, z, i),
            device_id={"sub": other},
            device_id_type=MESH,
        )

    panel_local = pltpu.make_async_copy(lfac_ref, panel.at[sub], psem.at[0])
    panel_across = pltpu.make_async_remote_copy(
        src_ref=lfac_ref,
        dst_ref=panel.at[sub],
        send_sem=psem.at[1],
        recv_sem=psem.at[2],
        device_id={"sub": other},
        device_id_type=MESH,
    )
    dinv_local = pltpu.make_async_copy(dinv_ref, dinv, psem.at[3])
    terms_across = pltpu.make_async_remote_copy(
        src_ref=outgoing,
        dst_ref=incoming,
        send_sem=tsem.at[0],
        recv_sem=tsem.at[1],
        device_id={"sub": other},
        device_id_type=MESH,
    )

    at_home = ours(z)

    def each_own(action):
        for top, count in ((True, top_count), (False, low_count)):
            @pl.loop(0, count)
            def _(i):
                @pl.when(jnp.logical_and(valid(top, z, i), owner(top, i) == sub))
                def _():
                    action(top, i)

    @pl.when(at_home)
    def _():
        each_own(lambda top, piece: own_local(top, piece).start())

    barrier = pltpu.get_barrier_semaphore()
    pl.semaphore_signal(barrier, inc=1, device_id={"sub": other}, device_id_type=MESH)

    @pl.when(z > 0)
    def _():
        pl.semaphore_signal(barrier, inc=1, device_id={"row": z - 1}, device_id_type=MESH)

    @pl.when(z < chips - 1)
    def _():
        pl.semaphore_signal(barrier, inc=1, device_id={"row": z + 1}, device_id_type=MESH)

    pl.semaphore_wait(barrier, 1 + jnp.where(z > 0, 1, 0) + jnp.where(z < chips - 1, 1, 0))

    @pl.when(jnp.logical_not(at_home))
    def _():
        each_own(lambda top, piece: own_across(top, piece).start())

    def arrived(top, chunk, i):
        where = place(top, sub, chunk, i)
        pltpu.make_async_copy(where, where, arrival(top, chunk, i)).wait()

    def spread(top, i, origin):
        @pl.when(z < chips - 1)
        def _():
            hop(top, z, i, 1, origin).start()

        @pl.when(z > 0)
        def _():
            hop(top, z, i, -1, origin).start()

    @pl.when(at_home)
    def _():
        each_own(lambda top, i: spread(top, i, source(top, i)))

        for top, count in ((True, top_count), (False, low_count)):
            @pl.loop(0, count)
            def _(i):
                @pl.when(jnp.logical_and(valid(top, z, i), owner(top, i) != sub))
                def _():
                    arrived(top, z, i)
                    spread(top, i, None)

        each_own(lambda top, i: arrived(top, z, i))

    panel_local.start()
    panel_across.start()
    dinv_local.start()

    def relay(top, t, i):
        up = z - t
        down = z + t

        @pl.when(jnp.logical_and(jnp.logical_and(up >= 0, ours(up)), valid(top, up, i)))
        def _():
            arrived(top, up, i)

            @pl.when(z < chips - 1)
            def _():
                hop(top, up, i, 1).start()

        @pl.when(jnp.logical_and(jnp.logical_and(down < chips, ours(down)), valid(top, down, i)))
        def _():
            arrived(top, down, i)

            @pl.when(z > 0)
            def _():
                hop(top, down, i, -1).start()

    panel_local.wait()

    @pl.loop(0, supers)
    def _(s):
        turned[s] = panel[sub, s].reshape(slots * width, width).T

    panel_across.wait()

    def multiply(table, first, s):
        rows = [
            jnp.maximum(anc_ref[sub * slots + i, s] - base, 0) for i in range(slots)
        ]
        ids = [anc_ref[first * slots + j, s] for j in range(slots)]
        if first:
            ids = [jnp.maximum(b - (NANC - slots), 0) for b in ids]
        total = None
        for j in range(0, slots, 2):
            left = jnp.concatenate(
                [
                    jnp.concatenate([table[row, ids[j]], table[row, ids[j + 1]]], axis=1)
                    for row in rows
                ],
                axis=0,
            )
            right = panel[first, s, pl.ds(j, 2)].reshape(2 * width, width)
            part = jnp.dot(left, right, preferred_element_type=jnp.float32)
            total = part if total is None else total + part
        return total

    first_mine = sub * lower
    last_mine = jnp.where(sub == 0, lower, chips) - 1
    final = jnp.maximum(jnp.maximum(z - first_mine, last_mine - z), 1)
    share = -(-supers // low_count)

    @pl.loop(1, chips)
    def _(t):
        @pl.loop(0, top_count)
        def _(i):
            relay(True, t, i)

        @pl.loop(0, low_count)
        def _(i):
            @pl.when(t == final)
            def _():
                @pl.loop(0, share)
                def _(k):
                    s = i * share + k

                    @pl.when(s < supers)
                    def _():
                        partial[s] = multiply(tops, 1, s)

            relay(False, t, i)

    def work(s):
        made = (-(partial[s] + multiply(lows, 0, s))).astype(jnp.bfloat16)
        inv_ref[s] = made.reshape(slots, width, width)
        return jnp.dot(turned[s], made, preferred_element_type=jnp.float32)

    together = 3 if half % 3 == 0 else 1

    @pl.loop(0, half // together)
    def _(m):
        for u in range(together):
            n = m * together + u
            outgoing[n] = work(n + other * half).astype(jnp.bfloat16)

    terms_across.start()

    @pl.loop(0, half // together)
    def _(m):
        for u in range(together):
            n = m * together + u
            kept[n] = work(n + sub * half)

    dinv_local.wait()
    terms_across.wait()
    diag_ref[...] = dinv[...] - (kept[...] + incoming[...].astype(jnp.float32))

    @pl.when(jnp.logical_not(at_home))
    def _():
        each_own(lambda top, piece: own_across(top, piece).wait_send())

    @pl.loop(0, chips)
    def _(t):
        up = z - t
        down = z + t
        go_up = jnp.logical_and(jnp.logical_and(up >= 0, ours(up)), z < chips - 1)
        go_down = jnp.logical_and(jnp.logical_and(down < chips, ours(down)), z > 0)
        for top, count in ((True, top_count), (False, low_count)):
            @pl.loop(0, count)
            def _(i):
                @pl.when(jnp.logical_and(go_up, valid(top, up, i)))
                def _():
                    hop(top, up, i, 1).wait_send()

                @pl.when(jnp.logical_and(go_down, valid(top, down, i)))
                def _():
                    hop(top, down, i, -1).wait_send()


def shards(chips, ainv, lfac, anc, dinv):
    supers, slots, width, _ = lfac.shape
    owned = ainv.shape[1]
    held = min(owned, NANC)
    pieces = 2 * (owned // held)
    kept_rows = (NANC - slots) * NANC
    half = supers // 2
    vmem = pl.BlockSpec(memory_space=pltpu.VMEM)
    hbm = pl.BlockSpec(memory_space=pltpu.HBM)
    return pl.pallas_call(
        functools.partial(kernel, chips),
        out_shape=(
            pltpu.VMEM(lfac.shape, jnp.bfloat16),
            pltpu.VMEM(dinv.shape, jnp.float32),
        ),
        in_specs=[pl.BlockSpec(memory_space=pltpu.SMEM), hbm, hbm, hbm],
        out_specs=(vmem, vmem),
        scratch_shapes=[
            pltpu.VMEM((NANC - slots, slots, width, width), jnp.bfloat16),
            pltpu.VMEM((NANC - slots, NANC - slots, width, width), jnp.bfloat16),
            pltpu.VMEM((2, supers, slots, width, width), jnp.bfloat16),
            pltpu.VMEM((supers, width, slots * width), jnp.bfloat16),
            pltpu.VMEM((supers, slots * width, width), jnp.float32),
            pltpu.VMEM(dinv.shape, jnp.float32),
            pltpu.VMEM((half, width, width), jnp.bfloat16),
            pltpu.VMEM((half, width, width), jnp.bfloat16),
            pltpu.VMEM((half, width, width), jnp.float32),
            pltpu.SemaphoreType.DMA((chips, 2)),
            pltpu.SemaphoreType.DMA((chips, pieces)),
            pltpu.SemaphoreType.DMA((2, chips, 2)),
            pltpu.SemaphoreType.DMA((2, chips, pieces)),
            pltpu.SemaphoreType.DMA((4,)),
            pltpu.SemaphoreType.DMA((2,)),
        ],
        compiler_params=pltpu.CompilerParams(
            collective_id=0, has_side_effects=True, vmem_limit_bytes=60 * 1024 * 1024
        ),
        cost_estimate=pl.CostEstimate(
            flops=2 * supers * slots * (2 * slots + 1) * width**3,
            bytes_accessed=2 * (kept_rows + 4 * supers * slots) * width**2,
            transcendentals=0,
        ),
    )(anc.T, ainv.reshape(owned // held, held, width, width), lfac, dinv)


def solution(mesh):
    return jax.shard_map(
        functools.partial(shards, mesh.shape["row"]),
        mesh=mesh,
        in_specs=(
            P(("pole", "col"), ("row", "sub"), None, None),
            P(("pole", "row", "col"), "sub", None, None),
            P(("row", "col"), None),
            P(("pole", "row", "col", "sub"), None, None),
        ),
        out_specs=(
            P(("pole", "row", "col"), "sub", None, None),
            P(("pole", "row", "col", "sub"), None, None),
        ),
        check_vma=False,
    )
```

```python
import functools

import jax
import jax.numpy as jnp
from jax import lax
from jax.experimental import pallas as pl
from jax.experimental.pallas import tpu as pltpu
from jax.sharding import PartitionSpec as P

NANC = 16
MESH = pl.DeviceIdType.MESH


def kernel(
    chips, anc_ref, ainv_ref, lfac_ref, dinv_ref, inv_ref, diag_ref,
    tops, lows, panel, turned, partial, dinv, outgoing, incoming, kept,
    recv_top, recv_low, send_top, send_low, psem, tsem,
):
    z = lax.axis_index("row")
    sub = lax.axis_index("sub")
    other = 1 - sub
    supers, slots, width, _ = lfac_ref.shape
    half = supers // 2
    quarters = NANC // slots
    split = NANC - slots
    lower = chips * split // NANC
    base = sub * split
    owned_rows, held, _, _ = ainv_ref.shape
    whole = held == NANC
    top_count = 2
    low_count = 2

    def valid(top, chunk, i):
        if whole:
            return True
        last = lax.rem(chunk * 2 + i, quarters) == quarters - 1
        return last if top else jnp.logical_not(last)

    def owner(top, i):
        return i

    def ours(chunk):
        return jnp.where(sub == 0, chunk < lower, chunk >= lower)

    def place(top, core, chunk, i):
        if whole:
            row = chunk * 2 * owned_rows - core * split
            if top:
                return tops.at[pl.ds(row + i * owned_rows, owned_rows)]
            return lows.at[pl.ds(row + i * owned_rows, owned_rows)]
        quarter = chunk * 2 + i
        row = lax.div(quarter, quarters) - core * split
        if top:
            return tops.at[pl.ds(row, 1)]
        return lows.at[pl.ds(row, 1), pl.ds(lax.rem(quarter, quarters) * slots, slots)]

    def source(top, i):
        if not whole:
            return ainv_ref
        if top:
            return ainv_ref.at[:, pl.ds(split, slots)]
        return ainv_ref.at[:, pl.ds(0, split)]

    def arrival(top, chunk, i):
        return (recv_top if top else recv_low).at[chunk, i]

    def departure(top, step, chunk, i):
        return (send_top if top else send_low).at[0 if step > 0 else 1, chunk, i]

    def hop(top, chunk, i, step, origin=None):
        where = place(top, sub, chunk, i)
        return pltpu.make_async_remote_copy(
            src_ref=where if origin is None else origin,
            dst_ref=where,
            send_sem=departure(top, step, chunk, i),
            recv_sem=arrival(top, chunk, i),
            device_id={"row": z + step},
            device_id_type=MESH,
        )

    def own_local(top, i):
        return pltpu.make_async_copy(
            source(top, i), place(top, sub, z, i), arrival(top, z, i)
        )

    def own_across(top, i):
        return pltpu.make_async_remote_copy(
            src_ref=source(top, i),
            dst_ref=place(top, other, z, i),
            send_sem=departure(top, 1, z, i),
            recv_sem=arrival(top, z, i),
            device_id={"sub": other},
            device_id_type=MESH,
        )

    panel_local = pltpu.make_async_copy(lfac_ref, panel.at[sub], psem.at[0])
    panel_across = pltpu.make_async_remote_copy(
        src_ref=lfac_ref,
        dst_ref=panel.at[sub],
        send_sem=psem.at[1],
        recv_sem=psem.at[2],
        device_id={"sub": other},
        device_id_type=MESH,
    )
    dinv_local = pltpu.make_async_copy(dinv_ref, dinv, psem.at[3])
    terms_across = pltpu.make_async_remote_copy(
        src_ref=outgoing,
        dst_ref=incoming,
        send_sem=tsem.at[0],
        recv_sem=tsem.at[1],
        device_id={"sub": other},
        device_id_type=MESH,
    )

    at_home = ours(z)

    def each_own(action):
        for top, count in ((True, top_count), (False, low_count)):
            @pl.loop(0, count)
            def _(i):
                @pl.when(jnp.logical_and(valid(top, z, i), owner(top, i) == sub))
                def _():
                    action(top, i)

    @pl.when(at_home)
    def _():
        each_own(lambda top, piece: own_local(top, piece).start())

    barrier = pltpu.get_barrier_semaphore()
    pl.semaphore_signal(barrier, inc=1, device_id={"sub": other}, device_id_type=MESH)

    @pl.when(z > 0)
    def _():
        pl.semaphore_signal(barrier, inc=1, device_id={"row": z - 1}, device_id_type=MESH)

    @pl.when(z < chips - 1)
    def _():
        pl.semaphore_signal(barrier, inc=1, device_id={"row": z + 1}, device_id_type=MESH)

    pl.semaphore_wait(barrier, 1 + jnp.where(z > 0, 1, 0) + jnp.where(z < chips - 1, 1, 0))

    @pl.when(jnp.logical_not(at_home))
    def _():
        each_own(lambda top, piece: own_across(top, piece).start())

    def arrived(top, chunk, i):
        where = place(top, sub, chunk, i)
        pltpu.make_async_copy(where, where, arrival(top, chunk, i)).wait()

    def spread(top, i, origin):
        @pl.when(z < chips - 1)
        def _():
            hop(top, z, i, 1, origin).start()

        @pl.when(z > 0)
        def _():
            hop(top, z, i, -1, origin).start()

    @pl.when(at_home)
    def _():
        each_own(lambda top, i: spread(top, i, source(top, i)))

        for top, count in ((True, top_count), (False, low_count)):
            @pl.loop(0, count)
            def _(i):
                @pl.when(jnp.logical_and(valid(top, z, i), owner(top, i) != sub))
                def _():
                    arrived(top, z, i)
                    spread(top, i, None)

        each_own(lambda top, i: arrived(top, z, i))

    panel_local.start()
    panel_across.start()
    dinv_local.start()

    def relay(top, t, i):
        up = z - t
        down = z + t

        @pl.when(jnp.logical_and(jnp.logical_and(up >= 0, ours(up)), valid(top, up, i)))
        def _():
            arrived(top, up, i)

            @pl.when(z < chips - 1)
            def _():
                hop(top, up, i, 1).start()

        @pl.when(jnp.logical_and(jnp.logical_and(down < chips, ours(down)), valid(top, down, i)))
        def _():
            arrived(top, down, i)

            @pl.when(z > 0)
            def _():
                hop(top, down, i, -1).start()

    panel_local.wait()

    @pl.loop(0, supers)
    def _(s):
        turned[s] = panel[sub, s].reshape(slots * width, width).T

    panel_across.wait()

    def multiply(table, first, s):
        rows = [
            jnp.maximum(anc_ref[sub * slots + i, s] - base, 0) for i in range(slots)
        ]
        ids = [anc_ref[first * slots + j, s] for j in range(slots)]
        if first:
            ids = [jnp.maximum(b - (NANC - slots), 0) for b in ids]
        total = None
        for j in range(0, slots, 2):
            left = jnp.concatenate(
                [
                    jnp.concatenate([table[row, ids[j]], table[row, ids[j + 1]]], axis=1)
                    for row in rows
                ],
                axis=0,
            )
            right = panel[first, s, pl.ds(j, 2)].reshape(2 * width, width)
            part = jnp.dot(left, right, preferred_element_type=jnp.float32)
            total = part if total is None else total + part
        return total

    first_mine = sub * lower
    last_mine = jnp.where(sub == 0, lower, chips) - 1
    final = jnp.maximum(jnp.maximum(z - first_mine, last_mine - z), 1)
    share = -(-supers // low_count)

    @pl.loop(1, chips)
    def _(t):
        @pl.loop(0, top_count)
        def _(i):
            relay(True, t, i)

        @pl.loop(0, low_count)
        def _(i):
            @pl.when(t == final)
            def _():
                @pl.loop(0, share)
                def _(k):
                    s = i * share + k

                    @pl.when(s < supers)
                    def _():
                        partial[s] = multiply(tops, 1, s)

            relay(False, t, i)

    def work(s):
        made = (-(partial[s] + multiply(lows, 0, s))).astype(jnp.bfloat16)
        inv_ref[s] = made.reshape(slots, width, width)
        return jnp.dot(turned[s], made, preferred_element_type=jnp.float32)

    together = 6 if half % 6 == 0 else 1

    @pl.loop(0, half // together)
    def _(m):
        for u in range(together):
            n = m * together + u
            outgoing[n] = work(n + other * half).astype(jnp.bfloat16)

    terms_across.start()

    @pl.loop(0, half // together)
    def _(m):
        for u in range(together):
            n = m * together + u
            kept[n] = work(n + sub * half)

    dinv_local.wait()
    terms_across.wait()
    diag_ref[...] = dinv[...] - (kept[...] + incoming[...].astype(jnp.float32))

    @pl.when(jnp.logical_not(at_home))
    def _():
        each_own(lambda top, piece: own_across(top, piece).wait_send())

    @pl.loop(0, chips)
    def _(t):
        up = z - t
        down = z + t
        go_up = jnp.logical_and(jnp.logical_and(up >= 0, ours(up)), z < chips - 1)
        go_down = jnp.logical_and(jnp.logical_and(down < chips, ours(down)), z > 0)
        for top, count in ((True, top_count), (False, low_count)):
            @pl.loop(0, count)
            def _(i):
                @pl.when(jnp.logical_and(go_up, valid(top, up, i)))
                def _():
                    hop(top, up, i, 1).wait_send()

                @pl.when(jnp.logical_and(go_down, valid(top, down, i)))
                def _():
                    hop(top, down, i, -1).wait_send()


def shards(chips, ainv, lfac, anc, dinv):
    supers, slots, width, _ = lfac.shape
    owned = ainv.shape[1]
    held = min(owned, NANC)
    pieces = 2
    kept_rows = (NANC - slots) * NANC
    half = supers // 2
    vmem = pl.BlockSpec(memory_space=pltpu.VMEM)
    hbm = pl.BlockSpec(memory_space=pltpu.HBM)
    return pl.pallas_call(
        functools.partial(kernel, chips),
        out_shape=(
            pltpu.VMEM(lfac.shape, jnp.bfloat16),
            pltpu.VMEM(dinv.shape, jnp.float32),
        ),
        in_specs=[pl.BlockSpec(memory_space=pltpu.SMEM), hbm, hbm, hbm],
        out_specs=(vmem, vmem),
        scratch_shapes=[
            pltpu.VMEM((NANC - slots, slots, width, width), jnp.bfloat16),
            pltpu.VMEM((NANC - slots, NANC - slots, width, width), jnp.bfloat16),
            pltpu.VMEM((2, supers, slots, width, width), jnp.bfloat16),
            pltpu.VMEM((supers, width, slots * width), jnp.bfloat16),
            pltpu.VMEM((supers, slots * width, width), jnp.float32),
            pltpu.VMEM(dinv.shape, jnp.float32),
            pltpu.VMEM((half, width, width), jnp.bfloat16),
            pltpu.VMEM((half, width, width), jnp.bfloat16),
            pltpu.VMEM((half, width, width), jnp.float32),
            pltpu.SemaphoreType.DMA((chips, 2)),
            pltpu.SemaphoreType.DMA((chips, pieces)),
            pltpu.SemaphoreType.DMA((2, chips, 2)),
            pltpu.SemaphoreType.DMA((2, chips, pieces)),
            pltpu.SemaphoreType.DMA((4,)),
            pltpu.SemaphoreType.DMA((2,)),
        ],
        compiler_params=pltpu.CompilerParams(
            collective_id=0, has_side_effects=True, vmem_limit_bytes=60 * 1024 * 1024
        ),
        cost_estimate=pl.CostEstimate(
            flops=2 * supers * slots * (2 * slots + 1) * width**3,
            bytes_accessed=2 * (kept_rows + 4 * supers * slots) * width**2,
            transcendentals=0,
        ),
    )(anc.T, ainv.reshape(owned // held, held, width, width), lfac, dinv)


def solution(mesh):
    return jax.shard_map(
        functools.partial(shards, mesh.shape["row"]),
        mesh=mesh,
        in_specs=(
            P(("pole", "col"), ("row", "sub"), None, None),
            P(("pole", "row", "col"), "sub", None, None),
            P(("row", "col"), None),
            P(("pole", "row", "col", "sub"), None, None),
        ),
        out_specs=(
            P(("pole", "row", "col"), "sub", None, None),
            P(("pole", "row", "col", "sub"), None, None),
        ),
        check_vma=False,
    )
```
